32 devices in a mesh: dp: 16 (over z, x, core), tensor: 2 (over y).
Axes of the slice: x: 2, y: 2, z: 4, core: 2. Of those that a mesh axis runs over, the one named last changes fastest.
Arguments:
- layer_input: bfloat16 [16384, 1024], P('dp'), may hold values from -24 to 24
- amplitude: float32 [1024], replicated, may hold values from 0.5 to 1.5
- expansion: bfloat16 [1024, 2, 2048], P(None, None, 'tensor'), may hold values from -0.1875 to 0.1875
- timescale: bfloat16 [1024, 32], P(None, 'tensor'), may hold values from -0.375 to 0.375
- selection: bfloat16 [1024, 2, 128], replicated, may hold values from -0.1875 to 0.1875
- smoothing: float32 [4, 2048], P(None, 'tensor'), may hold values from -3 to 3
- baseline: float32 [2048], P('tensor'), may hold values from -3 to 3
- blending: float32 [4, 2, 128], replicated, may hold values from -3 to 3
- pedestal: float32 [2, 128], replicated, may hold values from -3 to 3
- offset: float32 [32], P('tensor'), may hold values from -6.9 to -2.3
- retention: float32 [32], P('tensor'), may hold values from 0 to 2.77
- passthrough: float32 [32], P('tensor'), may hold values from 0.1 to 1.9
- emphasis: float32 [2048], P('tensor'), may hold values from 0.5 to 1.5
- readout: bfloat16 [2048, 1024], P('tensor'), may hold values from -0.125 to 0.125
- cotangent: bfloat16 [16384, 1024], P('dp'), may hold values from -6 to 6
Outputs:
- layer_output: bfloat16 [16384, 1024], P('dp')
- input_gradient: bfloat16 [16384, 1024], P('dp')
- amplitude_gradient: float32 [1024], replicated
- expansion_gradient: float32 [1024, 2, 2048], P(None, None, 'tensor')
- timescale_gradient: float32 [1024, 32], P(None, 'tensor')
- selection_gradient: float32 [1024, 2, 128], replicated
- smoothing_gradient: float32 [4, 2048], P(None, 'tensor')
- baseline_gradient: float32 [2048], P('tensor')
- blending_gradient: float32 [4, 2, 128], replicated
- pedestal_gradient: float32 [2, 128], replicated
- offset_gradient: float32 [32], P('tensor')
- retention_gradient: float32 [32], P('tensor')
- passthrough_gradient: float32 [32], P('tensor')
- emphasis_gradient: float32 [2048], P('tensor')
- readout_gradient: float32 [2048, 1024], P('tensor')
The draws below stay inside these ranges and needn't reach their ends.
All inputs are finite; a program needn't handle non-finite values.
Results may differ from the reference program's by a relative error of at most 0.025.
Values may be sent and summed in bfloat16 or wider, within the bound.
A program may use at most 192 MiB of HBM per device.

```python
import math
import jax
import jax.numpy as jnp
from jax import lax

D = 1024
NH = 32
HEAD = 64
STATE = 128
SPAN = 256
KCONV = 4
LEN = 1024
DI = 2048
TOKENS = 16384


def draw_layer_input(key, part):
    key = jax.random.fold_in(key, 5)
    sample_key, row_key, column_key = jax.random.split(key, 3)
    samples = jnp.clip(jax.random.normal(sample_key, (TOKENS, D), jnp.float32), -4.0, 4.0)
    row_scale = jnp.exp(jax.random.uniform(row_key, (TOKENS, 1), jnp.float32, math.log(0.3), math.log(3.0)))
    column_scale = jnp.exp(jax.random.uniform(column_key, (1, D), jnp.float32, math.log(0.5), math.log(2.0)))
    return (samples * row_scale * column_scale).astype(jnp.bfloat16)


def level_of(key, extent, cuts, smallest, largest):
    gain = 1.0
    for axis_at, parts in cuts:
        heights = jax.random.uniform(jax.random.fold_in(jax.random.fold_in(key, 6), axis_at), (parts,), jnp.float32, smallest / len(cuts), largest / len(cuts))
        gain = gain * jnp.repeat(jnp.exp(heights), extent[axis_at] // parts).reshape((-1,) + (1,) * (len(extent) - 1 - axis_at))
    return gain


def centred(own_key, extent, scale, limit, cuts=(), held_as=jnp.bfloat16):
    values = scale * jax.random.normal(own_key, extent, jnp.float32)
    if cuts:
        values = values * level_of(own_key, extent, cuts, -0.22, 0.18)
    return jnp.clip(values, -limit, limit).astype(held_as)


def setup_inputs(seed: int = 0) -> dict:
    arg_keys = jax.random.split(jax.random.key(seed), 16)
    return {
        "layer_input": draw_layer_input(jax.random.fold_in(arg_keys[15], 71), 0),
        "amplitude": jnp.clip(1.0 + 0.1 * jax.random.normal(arg_keys[1], (D,), jnp.float32), 0.5, 1.5),
        "expansion": centred(arg_keys[2], (D, 2, DI), D ** -0.5, 0.1875, ((2, 2),)),
        "timescale": centred(arg_keys[3], (D, NH), (D // 4) ** -0.5, 0.375, ((1, 2),)),
        "selection": centred(arg_keys[4], (D, 2, STATE), D ** -0.5, 0.1875),
        "smoothing": centred(arg_keys[5], (KCONV, DI), 0.5, 3.0, ((1, 2),), jnp.float32),
        "baseline": centred(arg_keys[6], (DI,), 0.5, 3.0, ((0, 2),), jnp.float32),
        "blending": centred(arg_keys[7], (KCONV, 2, STATE), 0.5, 3.0, (), jnp.float32),
        "pedestal": centred(arg_keys[8], (2, STATE), 0.5, 3.0, (), jnp.float32),
        "offset": jnp.clip(-6.9 + 4.6000001430511475 * jax.random.uniform(arg_keys[9], (NH,), jnp.float32) ** level_of(arg_keys[9], (NH,), ((0, 2),), -0.2, 0.2), -6.9, -2.3),
        "retention": jnp.clip(2.77 * jax.random.uniform(arg_keys[10], (NH,), jnp.float32) ** level_of(arg_keys[10], (NH,), ((0, 2),), -0.2, 0.2), 0.0, 2.77),
        "passthrough": jnp.clip(1.0 + 0.18 * jax.random.normal(arg_keys[11], (NH,), jnp.float32), 0.1, 1.9),
        "emphasis": jnp.clip(1.0 + 0.1 * jax.random.normal(arg_keys[12], (DI,), jnp.float32), 0.5, 1.5),
        "readout": centred(arg_keys[13], (DI, D), (NH * HEAD) ** -0.5, 0.125, ((0, 2),)),
        "cotangent": centred(arg_keys[14], (TOKENS, D), 1.0, 6.0, ((0, 16),)),
    }


epsilon = 1e-05
highest = lax.Precision.HIGHEST

@jax.custom_vjp
def low(v):
    return lax.optimization_barrier(v.astype(jnp.bfloat16)).astype(jnp.float32)

@jax.custom_vjp
def low_back(v):
    return v

def low_keep(v):
    return (low(v), None)

def low_pass(kept, grad):
    return (grad,)

def back_keep(v):
    return (v, None)

def back_low(kept, grad):
    return (low(grad),)
low.defvjp(low_keep, low_pass)
low_back.defvjp(back_keep, back_low)

def causal_conv(values, kernel, shift_term):
    length = values.shape[0]
    padded = jnp.pad(values, [(KCONV - 1, 0)] + [(0, 0)] * (values.ndim - 1))
    summed = shift_term + kernel[0] * padded[0:length]
    for tap_index in range(1, KCONV):
        summed = summed + kernel[tap_index] * padded[tap_index:tap_index + length]
    return jax.nn.silu(summed)

def span_terms(scores, log_decay, timestep):
    cumulative = jnp.cumsum(log_decay, axis=-2)
    length = log_decay.shape[-2]
    causal = (jnp.arange(length)[:, None] >= jnp.arange(length)[None, :])[:, :, None]
    spread = cumulative[..., :, None, :] - cumulative[..., None, :, :]
    decay_factor = jnp.where(causal, jnp.exp(jnp.where(causal, spread, 0.0)), 0.0)
    mixing = scores[..., None] * decay_factor * timestep[..., None, :, :]
    growth = jnp.exp(cumulative)
    block_end = cumulative[..., -1:, :]
    weights_in = jnp.exp(block_end - cumulative) * timestep
    carried = jnp.exp(block_end[..., 0, :])
    return (mixing, growth, weights_in, carried)

def span_step(carry_state, pieces):
    inner_block, input_map, output_map, decay_block, step_block = pieces
    scores = low_back(jnp.dot(output_map, input_map.T, precision=highest))
    mixing, growth, weights_in, carried = span_terms(scores, decay_block, step_block)
    mixing = low(mixing)
    diagonal_term = jnp.einsum('tuh,uhp->thp', mixing, inner_block, precision=highest)
    state_low = low(carry_state)
    readout_term = low_back(jnp.einsum('tn,hnp->thp', output_map, state_low, precision=highest))
    weighted = low(inner_block * weights_in[..., None])
    produced = low_back(jnp.einsum('un,uhp->hnp', input_map, weighted, precision=highest))
    next_state = carried[..., None, None] * carry_state + produced
    output = diagonal_term + growth[..., None] * readout_term
    return (next_state, output)

def layer(seq_input, amplitude, expansion, timescale, selection, smoothing, baseline, blending, pedestal, offset, retention, passthrough, emphasis, readout):
    variance = lax.optimization_barrier(jnp.mean(seq_input * seq_input, axis=-1, keepdims=True))
    normed = low(seq_input * lax.rsqrt(variance + epsilon) * amplitude)
    gate_inner = low_back(jnp.einsum('ld,dkc->lkc', normed, expansion, precision=highest))
    raw_step = low_back(jnp.dot(normed, timescale, precision=highest))
    raw_select = low_back(jnp.einsum('ld,dkn->lkn', normed, selection, precision=highest))
    inner_act = low(causal_conv(gate_inner[:, 1], smoothing, baseline))
    select_act = low(causal_conv(raw_select, blending, pedestal))
    timestep = jax.nn.softplus(raw_step + offset)
    log_decay = -timestep * jnp.exp(retention)
    length = seq_input.shape[0]
    spans = length // SPAN
    inner_heads = inner_act.reshape(spans, SPAN, NH, HEAD)
    input_maps = select_act[:, 0].reshape(spans, SPAN, STATE)
    output_maps = select_act[:, 1].reshape(spans, SPAN, STATE)
    initial_state = jnp.zeros((NH, STATE, HEAD), jnp.float32)
    final_state, outputs = lax.scan(jax.checkpoint(span_step), initial_state, (inner_heads, input_maps, output_maps, log_decay.reshape(spans, SPAN, NH), timestep.reshape(spans, SPAN, NH)))
    mixed = outputs.reshape(length, NH, HEAD) + passthrough[:, None] * inner_act.reshape(length, NH, HEAD)
    mixed = low_back(mixed.reshape(length, NH * HEAD))
    gated = mixed * jax.nn.silu(gate_inner[:, 0])
    inverse = lax.rsqrt(lax.optimization_barrier(jnp.mean(gated * gated, axis=-1, keepdims=True)) + epsilon)
    scaled = low(gated * emphasis)
    projected = low_back(jnp.dot(scaled, readout, precision=highest))
    return seq_input + inverse * projected

def reference(layer_input, amplitude, expansion, timescale, selection, smoothing, baseline, blending, pedestal, offset, retention, passthrough, emphasis, readout, cotangent):
    params = tuple((weight_array.astype(jnp.float32) for weight_array in (amplitude, expansion, timescale, selection, smoothing, baseline, blending, pedestal, offset, retention, passthrough, emphasis, readout)))
    sequences = layer_input.shape[0] // LEN
    inputs = layer_input.astype(jnp.float32).reshape(sequences, LEN, D)
    cotangents = cotangent.astype(jnp.float32).reshape(sequences, LEN, D)

    def per_sequence(totals, paired):
        seq_input, seq_cotangent = paired

        def bound(seq_values, weights):
            return layer(seq_values, weights[0], weights[1], weights[2], weights[3], weights[4], weights[5], weights[6], weights[7], weights[8], weights[9], weights[10], weights[11], weights[12])
        output, pullback = jax.vjp(bound, seq_input, params)
        input_part, weight_parts = pullback(seq_cotangent)
        totals = jax.tree.map(lambda first, second: first + second, totals, weight_parts)
        return (totals, (output, input_part))
    initial = jax.tree.map(jnp.zeros_like, params)
    totals, (outputs, input_parts) = lax.scan(per_sequence, initial, (inputs, cotangents))
    return (outputs.reshape(-1, D).astype(jnp.bfloat16), input_parts.reshape(-1, D).astype(jnp.bfloat16), totals[0], totals[1], totals[2], totals[3], totals[4], totals[5], totals[6], totals[7], totals[8], totals[9], totals[10], totals[11], totals[12])
```

```python
import jax
import jax.numpy as jnp
from jax import lax
from jax.experimental import pallas as pl
from jax.experimental.pallas import tpu as pltpu
from jax.sharding import PartitionSpec as P

NH = 32
HEAD = 64
STATE = 128
SPAN = 256
KCONV = 4
LEN = 1024


epsilon = 1e-05


def input_norm(values, amplitude):
    variance = jnp.mean(values * values, axis=-1, keepdims=True)
    return values * lax.rsqrt(variance + epsilon) * amplitude


def causal_conv(values, kernel, shift_term):
    length = values.shape[1]
    padded = jnp.pad(values, [(0, 0), (KCONV - 1, 0)] + [(0, 0)] * (values.ndim - 2))
    summed = shift_term + kernel[0] * padded[:, 0:length]
    for tap_index in range(1, KCONV):
        summed = summed + kernel[tap_index] * padded[:, tap_index : tap_index + length]
    return jax.nn.silu(summed)


def step_terms(raw_step, offset, retention):
    timestep = jax.nn.softplus(raw_step + offset)
    return (timestep, -timestep * jnp.exp(retention))


VMEM_BYTES = 56 * 1024 * 1024


def mm(left, right, left_axis, right_axis):
    return lax.dot_general(
        left, right, (((left_axis,), (right_axis,)), ((), ())), preferred_element_type=jnp.float32
    )


def expand(per_head, spread_map):
    high = per_head.astype(jnp.bfloat16)
    low = (per_head - high.astype(jnp.float32)).astype(jnp.bfloat16)
    return mm(high, spread_map, 1, 0) + mm(low, spread_map, 1, 0)


def collect(per_channel, spread_map):
    high = per_channel.astype(jnp.bfloat16)
    low = (per_channel - high.astype(jnp.float32)).astype(jnp.bfloat16)
    return mm(high, spread_map, 1, 1) + mm(low, spread_map, 1, 1)


def sigmoid(values):
    return 1.0 / (1.0 + jnp.exp(-values))


def forward_kernel(
    spans,
    x_ref,
    z_ref,
    select_ref,
    cum_ref,
    step_ref,
    cum_row_ref,
    step_row_ref,
    channel_ref,
    spread_ref,
    readout_ref,
    cotangent_ref,
    pre_ref,
    mixed_ref,
    scaled_ref,
    entering_ref,
    back_ref,
    projected_ref,
    token_ref,
    padded,
    state,
):
    channels = x_ref.shape[1]
    heads = channels // HEAD
    step = pl.program_id(0)
    x = x_ref[...].astype(jnp.float32)

    @pl.when(lax.rem(step, spans) == 0)
    def _():
        state[...] = jnp.zeros_like(state)
        padded[0:8, :] = jnp.zeros((8, channels), jnp.float32)

    padded[8 : 8 + SPAN, :] = x
    pre = channel_ref[4:5, :] + channel_ref[3:4, :] * x
    for tap in range(KCONV - 1):
        pre = pre + channel_ref[tap : tap + 1, :] * padded[5 + tap : 5 + tap + SPAN, :]
    padded[0:8, :] = x[SPAN - 8 :, :]
    pre_low = pre.astype(jnp.bfloat16)
    pre_ref[...] = pre_low
    pre = pre_low.astype(jnp.float32)
    inner = (pre * sigmoid(pre)).astype(jnp.bfloat16)
    inner_float = inner.astype(jnp.float32)

    spread_map = spread_ref[...]
    input_map = select_ref[:, 0:STATE]
    output_map = select_ref[:, STATE:]
    cum = cum_ref[...]
    growth = expand(jnp.exp(cum), spread_map)
    weights_in = expand(jnp.exp(cum[SPAN - 1 :, :] - cum) * step_ref[...], spread_map)
    state_low = state[...].astype(jnp.bfloat16)
    entering_ref[...] = state_low
    mixed = growth * mm(output_map, state_low, 1, 0) + channel_ref[6:7, :] * inner_float
    weighted = (inner_float * weights_in).astype(jnp.bfloat16)
    state[...] = growth[SPAN - 1 :, :] * state[...] + mm(input_map, weighted, 0, 0)

    scores = mm(output_map, input_map, 1, 1)
    rows = lax.broadcasted_iota(jnp.int32, (SPAN, SPAN), 0)
    columns = lax.broadcasted_iota(jnp.int32, (SPAN, SPAN), 1)
    causal = rows >= columns
    first_half = lax.broadcasted_iota(jnp.int32, (1, 2 * HEAD), 1) < HEAD
    parts = []
    for pair in range(heads // 2):
        inner_pair = inner[:, pair * 2 * HEAD : (pair + 1) * 2 * HEAD]
        total = mixed[:, pair * 2 * HEAD : (pair + 1) * 2 * HEAD]
        for side in range(2):
            head = 2 * pair + side
            gap = cum[:, head : head + 1] - cum_row_ref[head : head + 1, :]
            decay = jnp.exp(jnp.where(causal, gap, -1e30))
            mixing = (scores * decay * step_row_ref[head : head + 1, :]).astype(jnp.bfloat16)
            keep = first_half if side == 0 else jnp.logical_not(first_half)
            own = jnp.where(keep, inner_pair, jnp.zeros_like(inner_pair))
            total = total + mm(mixing, own, 1, 0)
        parts.append(total)
    mixed = jnp.concatenate(parts, axis=1)
    mixed_ref[...] = mixed.astype(jnp.bfloat16)
    z = z_ref[...].astype(jnp.float32)
    gated = mixed * (z * sigmoid(z))
    scaled = (gated * channel_ref[5:6, :]).astype(jnp.bfloat16)
    scaled_ref[...] = scaled
    back = mm(cotangent_ref[...], readout_ref[...], 1, 1)
    back_ref[...] = back.astype(jnp.bfloat16)
    projected_ref[...] = mm(scaled, readout_ref[...], 1, 0).astype(jnp.bfloat16)
    token_ref[:, 0:1] = jnp.sum(gated * gated, axis=1, keepdims=True)
    token_ref[:, 1:2] = jnp.sum(scaled.astype(jnp.float32) * back, axis=1, keepdims=True)


def backward_kernel(
    spans,
    x_ref,
    z_ref,
    pre_ref,
    mixed_ref,
    back_ref,
    entering_ref,
    select_ref,
    cum_ref,
    step_ref,
    cum_row_ref,
    channel_ref,
    spread_ref,
    token_ref,
    x_grad_ref,
    select_grad_ref,
    head_ref,
    row_ref,
    carried_ref,
    sums_ref,
    padded,
    state_grad,
    scores_sum,
):
    channels = x_ref.shape[1]
    heads = channels // HEAD
    step = pl.program_id(0)

    @pl.when(step == 0)
    def _():
        sums_ref[...] = jnp.zeros_like(sums_ref)

    @pl.when(lax.rem(step, spans) == 0)
    def _():
        state_grad[...] = jnp.zeros_like(state_grad)
        padded[SPAN : SPAN + 8, :] = jnp.zeros((8, channels), jnp.float32)

    inverse = token_ref[:, 0:1]
    pull = token_ref[:, 1:2]
    head_ref[:, 3 * heads : 3 * heads + 1] = inverse
    z = z_ref[...].astype(jnp.float32)
    mixed = mixed_ref[...].astype(jnp.float32)
    z_sigmoid = sigmoid(z)
    z_silu = z * z_sigmoid
    gated = mixed * z_silu
    scaled_grad = inverse * back_ref[...].astype(jnp.float32)
    sums_ref[5:6, :] += jnp.sum(scaled_grad * gated, axis=0, keepdims=True)
    gated_grad = scaled_grad * channel_ref[5:6, :] - pull * gated
    mixed_grad = (gated_grad * z_silu).astype(jnp.bfloat16)
    grad_float = mixed_grad.astype(jnp.float32)

    pre = pre_ref[...].astype(jnp.float32)
    pre_sigmoid = sigmoid(pre)
    pre_silu = pre * pre_sigmoid
    inner = pre_silu.astype(jnp.bfloat16)
    inner_float = inner.astype(jnp.float32)
    sums_ref[6:7, :] += jnp.sum(grad_float * inner_float, axis=0, keepdims=True)

    spread_map = spread_ref[...]
    input_map = select_ref[:, 0:STATE]
    output_map = select_ref[:, STATE:]
    cum = cum_ref[...]
    growth = expand(jnp.exp(cum), spread_map)
    weights_in = expand(jnp.exp(cum[SPAN - 1 :, :] - cum) * step_ref[...], spread_map)
    state_low = entering_ref[...]
    weighted = (inner_float * weights_in).astype(jnp.bfloat16)
    grown = growth * grad_float
    readout_grad = grown.astype(jnp.bfloat16)
    head_ref[:, 0:heads] = collect(grown * mm(output_map, state_low, 1, 0), spread_map)
    output_map_grad = mm(readout_grad, state_low, 1, 1)
    produced = state_grad[...]
    produced_low = produced.astype(jnp.bfloat16)
    carried_ref[...] = jnp.broadcast_to(
        jnp.sum(produced * state_low.astype(jnp.float32), axis=0, keepdims=True), carried_ref.shape
    )
    input_map_grad = mm(weighted, produced_low, 1, 1)
    weighted_grad = mm(input_map, produced_low, 1, 0)
    head_ref[:, heads : 2 * heads] = collect(weighted_grad * inner_float, spread_map)
    state_grad[...] = growth[SPAN - 1 :, :] * produced + mm(output_map, readout_grad, 0, 0)
    inner_grad = weighted_grad * weights_in + channel_ref[6:7, :] * grad_float

    scores = mm(input_map, output_map, 1, 1)
    rows = lax.broadcasted_iota(jnp.int32, (SPAN, SPAN), 0)
    columns = lax.broadcasted_iota(jnp.int32, (SPAN, SPAN), 1)
    causal = columns >= rows
    first_half = lax.broadcasted_iota(jnp.int32, (1, 2 * HEAD), 1) < HEAD
    steps = step_ref[...]
    parts = []
    for pair in range(heads // 2):
        lanes = slice(pair * 2 * HEAD, (pair + 1) * 2 * HEAD)
        inner_pair = inner[:, lanes]
        grad_pair = mixed_grad[:, lanes]
        total = inner_grad[:, lanes]
        for side in range(2):
            head = 2 * pair + side
            keep = first_half if side == 0 else jnp.logical_not(first_half)
            own = jnp.where(keep, grad_pair, jnp.zeros_like(grad_pair))
            mixing_grad = mm(inner_pair, own, 1, 1)
            gap = cum_row_ref[head : head + 1, :] - cum[:, head : head + 1]
            decay = jnp.exp(jnp.where(causal, gap, -1e30)) * steps[:, head : head + 1]
            total = total + mm((scores * decay).astype(jnp.bfloat16), own, 1, 0)
            reached = mixing_grad * decay
            if head == 0:
                scores_sum[...] = reached
            else:
                scores_sum[...] += reached
            flow = reached * scores
            row_ref[head : head + 1, :] = jnp.sum(flow, axis=0, keepdims=True)
            head_ref[:, 2 * heads + head : 2 * heads + head + 1] = jnp.sum(
                flow, axis=1, keepdims=True
            )
        parts.append(total)
    inner_grad = jnp.concatenate(parts, axis=1)
    scores_low = scores_sum[...].astype(jnp.bfloat16)
    select_grad_ref[:, 0:STATE] = input_map_grad + mm(scores_low, output_map, 1, 0)
    select_grad_ref[:, STATE:] = output_map_grad + mm(scores_low, input_map, 0, 0)

    pre_grad = inner_grad * (pre_sigmoid + pre_silu * (1.0 - pre_sigmoid))
    padded[0:SPAN, :] = pre_grad
    x = x_ref[...].astype(jnp.float32)
    x_grad = channel_ref[3:4, :] * pre_grad
    sums_ref[3:4, :] += jnp.sum(x * pre_grad, axis=0, keepdims=True)
    sums_ref[4:5, :] += jnp.sum(pre_grad, axis=0, keepdims=True)
    for tap in range(KCONV - 1):
        shifted = padded[3 - tap : 3 - tap + SPAN, :]
        x_grad = x_grad + channel_ref[tap : tap + 1, :] * shifted
        sums_ref[tap : tap + 1, :] += jnp.sum(x * shifted, axis=0, keepdims=True)
    x_grad_ref[...] = x_grad.astype(jnp.bfloat16)
    padded[SPAN : SPAN + 8, :] = pre_grad[0:8, :]


def swap_sum(part):
    if lax.axis_size("tensor") == 2:
        other = lax.ppermute(part, "tensor", [(0, 1), (1, 0)])
        return part.astype(jnp.float32) + other.astype(jnp.float32)
    return lax.psum(part, "tensor").astype(jnp.float32)


def in_blocks(values):
    return values.reshape((-1, SPAN) + values.shape[1:])


def shards(
    layer_input,
    amplitude,
    expansion,
    timescale,
    selection,
    smoothing,
    baseline,
    blending,
    pedestal,
    offset,
    retention,
    passthrough,
    emphasis,
    readout,
    cotangent,
):
    low = jnp.bfloat16
    wide = jnp.float32
    row_count, width = layer_input.shape
    sequences = row_count // LEN
    spans = LEN // SPAN
    blocks = row_count // SPAN
    heads = timescale.shape[1]
    channels = expansion.shape[2]
    residual = layer_input.astype(wide)
    upstream = cotangent.astype(wide)
    inverse_in = lax.rsqrt(jnp.mean(residual * residual, axis=1, keepdims=True) + epsilon)
    normed = (residual * inverse_in * amplitude).astype(low)
    expand_z = expansion[:, 0]
    expand_x = expansion[:, 1]
    select_map = selection.reshape(width, 2 * STATE)
    gate_inner = jnp.einsum(
        "ld,dkc->klc", normed, expansion, preferred_element_type=wide
    ).astype(low)
    z = gate_inner[0]
    raw_step = mm(normed, timescale, 1, 0)
    raw_select = mm(normed, select_map, 1, 0)
    select_act, select_pullback = jax.vjp(
        causal_conv,
        raw_select.reshape(sequences, LEN, 2 * STATE),
        blending.reshape(KCONV, 2 * STATE),
        pedestal.reshape(2 * STATE),
    )
    select_low = select_act.astype(low).reshape(row_count, 2 * STATE)
    (timestep, log_decay), step_pullback = jax.vjp(step_terms, raw_step, offset, retention)
    order = jnp.arange(SPAN)
    up_to = (order[:, None] >= order[None, :]).astype(wide)
    cumulative = jnp.einsum(
        "tu,buh->bth", up_to, in_blocks(log_decay), precision=lax.Precision.HIGHEST
    ).reshape(row_count, heads)
    cumulative_rows = cumulative.T
    step_rows = timestep.T
    channel_rows = jnp.concatenate(
        [
            smoothing,
            baseline[None],
            emphasis[None],
            jnp.repeat(passthrough, HEAD)[None],
            jnp.zeros((1, channels), wide),
        ]
    )
    spread_map = jnp.repeat(jnp.eye(heads, dtype=low), HEAD, axis=1)

    def rows_at(columns):
        return pl.BlockSpec((SPAN, columns), lambda i: (i, 0))

    def whole(shape):
        return pl.BlockSpec(shape, lambda i: (0,) * len(shape))

    parameters = pltpu.CompilerParams(
        dimension_semantics=("arbitrary",), vmem_limit_bytes=VMEM_BYTES
    )
    pre, mixed, scaled, entering, back, projected_part, token_part = pl.pallas_call(
        lambda *refs: forward_kernel(spans, *refs),
        grid=(blocks,),
        in_specs=[
            pl.BlockSpec((None, SPAN, channels), lambda i: (1, i, 0)),
            pl.BlockSpec((None, SPAN, channels), lambda i: (0, i, 0)),
            rows_at(2 * STATE),
            rows_at(heads),
            rows_at(heads),
            pl.BlockSpec((heads, SPAN), lambda i: (0, i)),
            pl.BlockSpec((heads, SPAN), lambda i: (0, i)),
            whole((8, channels)),
            whole((heads, channels)),
            whole((channels, width)),
            rows_at(width),
        ],
        out_specs=[
            rows_at(channels),
            rows_at(channels),
            rows_at(channels),
            pl.BlockSpec((STATE, channels), lambda i: (i, 0)),
            rows_at(channels),
            rows_at(width),
            rows_at(2),
        ],
        out_shape=[
            jax.ShapeDtypeStruct((row_count, channels), low),
            jax.ShapeDtypeStruct((row_count, channels), low),
            jax.ShapeDtypeStruct((row_count, channels), low),
            jax.ShapeDtypeStruct((blocks * STATE, channels), low),
            jax.ShapeDtypeStruct((row_count, channels), low),
            jax.ShapeDtypeStruct((row_count, width), low),
            jax.ShapeDtypeStruct((row_count, 2), wide),
        ],
        scratch_shapes=[
            pltpu.VMEM((SPAN + 8, channels), wide),
            pltpu.VMEM((STATE, channels), wide),
        ],
        compiler_params=parameters,
        cost_estimate=pl.CostEstimate(
            flops=8 * row_count * channels * width, bytes_accessed=20 * row_count * width, transcendentals=0
        ),
    )(
        gate_inner, gate_inner, select_low, cumulative, timestep, cumulative_rows, step_rows,
        channel_rows, spread_map, readout, cotangent,
    )
    squares, inverse_grad = lax.psum((token_part[:, 0], token_part[:, 1]), "tensor")
    squares, inverse_grad, projected_part = lax.optimization_barrier(
        (squares, inverse_grad, projected_part)
    )
    inverse = lax.rsqrt(squares / (NH * HEAD) + epsilon)
    pull = inverse_grad * inverse * inverse * inverse / (NH * HEAD)
    projected = swap_sum(projected_part)
    readout_part = mm((scaled.astype(wide) * inverse[:, None]).astype(low), cotangent, 0, 0)
    z_wide = z.astype(wide)
    mixed_wide = mixed.astype(wide)
    z_sigmoid = sigmoid(z_wide)
    z_silu = z_wide * z_sigmoid
    gated_grad = (
        inverse[:, None] * back.astype(wide) * emphasis - pull[:, None] * mixed_wide * z_silu
    )
    gate_grad = (gated_grad * mixed_wide * (z_sigmoid + z_silu * (1.0 - z_sigmoid))).astype(low)
    readout_sum = lax.psum(readout_part.astype(low), "dp")
    z_part = mm(normed, gate_grad, 0, 0).astype(low)
    z_part, inverse, pull = lax.optimization_barrier((z_part, inverse, pull))

    def rows_back(columns):
        return pl.BlockSpec((SPAN, columns), lambda i: (blocks - 1 - i, 0))

    x_grad, select_grad, head_terms, flow_rows, carried_terms, channel_sums = (
        pl.pallas_call(
            lambda *refs: backward_kernel(spans, *refs),
            grid=(blocks,),
            in_specs=[
                pl.BlockSpec((None, SPAN, channels), lambda i: (1, blocks - 1 - i, 0)),
                pl.BlockSpec((None, SPAN, channels), lambda i: (0, blocks - 1 - i, 0)),
                rows_back(channels),
                rows_back(channels),
                rows_back(channels),
                pl.BlockSpec((STATE, channels), lambda i: (blocks - 1 - i, 0)),
                rows_back(2 * STATE),
                rows_back(heads),
                rows_back(heads),
                pl.BlockSpec((heads, SPAN), lambda i: (0, blocks - 1 - i)),
                whole((8, channels)),
                whole((heads, channels)),
                rows_back(2),
            ],
            out_specs=[
                rows_back(channels),
                rows_back(2 * STATE),
                rows_back(3 * heads + 1),
                pl.BlockSpec((heads, SPAN), lambda i: (0, blocks - 1 - i)),
                pl.BlockSpec((8, channels), lambda i: (blocks - 1 - i, 0)),
                whole((8, channels)),
            ],
            out_shape=[
                jax.ShapeDtypeStruct((row_count, channels), low),
                jax.ShapeDtypeStruct((row_count, 2 * STATE), wide),
                jax.ShapeDtypeStruct((row_count, 3 * heads + 1), wide),
                jax.ShapeDtypeStruct((heads, row_count), wide),
                jax.ShapeDtypeStruct((blocks * 8, channels), wide),
                jax.ShapeDtypeStruct((8, channels), wide),
            ],
            scratch_shapes=[
                pltpu.VMEM((SPAN + 8, channels), wide),
                pltpu.VMEM((STATE, channels), wide),
                pltpu.VMEM((SPAN, SPAN), wide),
            ],
            compiler_params=parameters,
            cost_estimate=pl.CostEstimate(
                flops=2 * row_count * channels * width, bytes_accessed=2 * row_count * width, transcendentals=0
            ),
        )(
            gate_inner, gate_inner, pre, mixed, back, entering, select_low, cumulative, timestep,
            cumulative_rows, channel_rows, spread_map, jnp.stack([inverse, pull], axis=1),
        )
    )
    layer_output = (residual + head_terms[:, 3 * heads :] * projected).astype(low)
    x_grad, layer_output, readout_sum, z_part = lax.optimization_barrier(
        (x_grad, layer_output, readout_sum, z_part)
    )
    z_sum = lax.psum(z_part, "dp")
    cum_blocks = in_blocks(cumulative)
    step_blocks = in_blocks(timestep)
    growth_term, weights_grad, flow_in = (
        in_blocks(head_terms[:, i * heads : (i + 1) * heads]) for i in range(3)
    )
    flow_out = in_blocks(flow_rows.T)
    to_end = jnp.exp(cum_blocks[:, -1:] - cum_blocks)
    weights_term = weights_grad * to_end * step_blocks
    carried_grad = jnp.sum(
        carried_terms.reshape(blocks, 8, heads, HEAD)[:, 0], axis=2
    ) * jnp.exp(cum_blocks[:, -1])
    at_end = carried_grad + jnp.sum(weights_term, axis=1)
    cumulative_grad = flow_out - flow_in + growth_term - weights_term
    decay_grad = (
        jnp.einsum("ut,buh->bth", up_to, cumulative_grad, precision=lax.Precision.HIGHEST)
        + at_end[:, None]
    )
    safe_step = jnp.where(step_blocks > 0.0, step_blocks, 1.0)
    step_grad = flow_in / safe_step + weights_grad * to_end
    raw_step_grad, offset_part, retention_part = step_pullback(
        (step_grad.reshape(row_count, heads), decay_grad.reshape(row_count, heads))
    )
    raw_select_grad, blending_part, pedestal_part = select_pullback(
        select_grad.reshape(sequences, LEN, 2 * STATE)
    )
    step_low = raw_step_grad.astype(low)
    select_grad_low = raw_select_grad.reshape(row_count, 2 * STATE).astype(low)
    x_part = mm(normed, x_grad, 0, 0)
    normed_grad = (
        mm(gate_grad, expand_z, 1, 1)
        + mm(x_grad, expand_x, 1, 1)
        + mm(step_low, timescale, 1, 1)
        + mm(select_grad_low, select_map, 1, 1)
    )
    amplitude_part = jnp.sum(normed_grad * (residual * inverse_in), axis=0)
    normed_part = normed_grad.astype(low)
    time_rows = width * heads // channels
    head_row = jnp.concatenate(
        [offset_part, retention_part, jnp.zeros((channels - 2 * heads,), wide)]
    )[None]
    own_part = jnp.concatenate(
        [
            x_part,
            mm(normed, step_low, 0, 0).reshape(time_rows, channels),
            channel_sums,
            head_row,
        ]
    ).astype(low)
    shared_part = swap_sum(
        jnp.concatenate(
            [
                mm(normed, select_grad_low, 0, 0),
                blending_part,
                pedestal_part[None],
                amplitude_part.reshape(-1, 2 * STATE),
            ]
        ).astype(low)
    ).astype(low)
    own_part, shared_part, z_sum, normed_part = lax.optimization_barrier(
        (own_part, shared_part, z_sum, normed_part)
    )
    own_sum, shared_sum = jax.tree.map(
        lambda part: part.astype(wide), lax.psum((own_part, shared_part), "dp")
    )
    normed_grad = swap_sum(normed_part)
    scaled_back = normed_grad * amplitude
    input_gradient = (
        upstream
        + inverse_in * scaled_back
        - residual
        * (inverse_in * inverse_in * inverse_in)
        * jnp.mean(scaled_back * residual, axis=1, keepdims=True)
    ).astype(low)
    small = own_sum[width + time_rows :]
    return (
        layer_output,
        input_gradient,
        shared_sum[width + KCONV + 1 :].reshape(width),
        jnp.stack([z_sum.astype(wide), own_sum[:width]], axis=1),
        own_sum[width : width + time_rows].reshape(width, heads),
        shared_sum[:width].reshape(width, 2, STATE),
        small[0:KCONV],
        small[4],
        shared_sum[width : width + KCONV].reshape(KCONV, 2, STATE),
        shared_sum[width + KCONV].reshape(2, STATE),
        small[8, :heads],
        small[8, heads : 2 * heads],
        jnp.sum(small[6].reshape(heads, HEAD), axis=1),
        small[5],
        readout_sum.astype(wide),
    )


def solution(mesh):
    return jax.shard_map(
        shards,
        mesh=mesh,
        in_specs=(
            P("dp", None),
            P(),
            P(None, None, "tensor"),
            P(None, "tensor"),
            P(),
            P(None, "tensor"),
            P("tensor"),
            P(),
            P(),
            P("tensor"),
            P("tensor"),
            P("tensor"),
            P("tensor"),
            P("tensor", None),
            P("dp", None),
        ),
        out_specs=(
            P("dp", None),
            P("dp", None),
            P(),
            P(None, None, "tensor"),
            P(None, "tensor"),
            P(),
            P(None, "tensor"),
            P("tensor"),
            P(),
            P(),
            P("tensor"),
            P("tensor"),
            P("tensor"),
            P("tensor"),
            P("tensor", None),
        ),
        check_vma=False,
    )
```
